256 devices in a mesh: row: 16 (over y, x), col: 16 (over z, core).
Axes of the slice: x: 4, y: 4, z: 8, core: 2. Of those that a mesh axis runs over, the one named last changes fastest.
Arguments:
- amplitudes: float32 [512, 576, 576], P('row', None, 'col'), may hold values from -6 to 6
- integrals: float32 [576, 576, 3, 576], P('row', 'col'), may hold values from -0.03125 to 0.03125
- virt_irrep: int32 [576], replicated, may hold values from 0 to 7
- occ_irrep: int32 [60], replicated, may hold values from 0 to 7
- pair_index: int32 [512, 2], replicated, may hold values from 0 to 59
Outputs:
- ladder: float32 [512, 3, 576], P('row', None, 'col')
The draws below stay inside these ranges and needn't reach their ends.
Inputs may be any that keep to these rules, and one draw needn't show every extreme that they name: `virt_irrep`: irrep labels of the virtual orbitals, in no particular order. `pair_index`: indices of occupied orbitals; pairs may repeat.
All inputs are finite; a program needn't handle non-finite values.
Results may differ from the reference program's by a relative error of at most 0.00011.
Values sent between devices are 32-bit elements; how exact they have to be, the bound alone decides.
No kernel may reach another device: no remote copies, remote signals or barrier semaphores. Data moves between devices by JAX's collectives and lax.ppermute only.
A program may use at most 128 MiB of HBM per device.

```python
import math
import jax
import jax.numpy as jnp
import numpy as np
from jax import lax

NV = 576
NO = 60
SLAB = 3
PAIRS = 512


def touch_ends(values, key, least, top_value):
    longest = values.shape.index(max(values.shape))
    spots = []
    for shift in (0, 1):
        where = [jax.random.randint(jax.random.fold_in(key, axis), (), 0, length) for axis, length in enumerate(values.shape)]
        where[longest] = (where[longest] + shift) % values.shape[longest]
        spots.append(tuple(where))
    return values.at[spots[0]].set(least).at[spots[1]].set(top_value)


def block_scale(own_key, shape, pieces, least, high):
    def one(axis_at, shards_of):
        heights = jax.random.uniform(jax.random.fold_in(jax.random.fold_in(own_key, 6), axis_at), (shards_of,), jnp.float32, least / len(pieces), high / len(pieces))
        return jnp.repeat(jnp.exp(heights), shape[axis_at] // shards_of).reshape((-1,) + (1,) * (len(shape) - axis_at - 1))

    factor_of = one(*pieces[0])
    for cut in pieces[1:]:
        factor_of = factor_of * one(*cut)
    return factor_of


def cumulative_ranks(number_of, skew):
    portions = [(1 << 20) // math.isqrt(standing ** skew) + 1 for standing in range(1, number_of + 1)]
    width = 1 + sum(portions) // (1 << 30)
    return np.cumsum(np.array([max(1, weight // width) for weight in portions]))


def skewed_ids(key, dims, amount, lean):
    grid = cumulative_ranks(amount, lean)
    lot = jax.random.randint(jax.random.fold_in(key, 1), dims, 0, int(grid[amount - 1]))
    standing = jnp.searchsorted(jnp.asarray(grid, jnp.int32), lot, side="right")
    return jax.random.permutation(jax.random.fold_in(key, 2), amount)[standing].astype(jnp.int32)


def scatter_about(rng, extent, scale, bound, cuts=(), held_as=jnp.bfloat16):
    level = block_scale(rng, extent, cuts, -0.22, 0.18) if cuts else 1.0
    result = jax.random.normal(rng, extent, jnp.float32) * scale * level
    return jnp.minimum(jnp.maximum(result, -bound), bound).astype(held_as)


def setup_inputs(seed: int = 0) -> dict:
    key_of = jax.random.split(jax.random.key(seed), 6)
    amplitudes = scatter_about(key_of[0], (PAIRS, NV, NV), 1.0, 6.0, ((0, 16), (2, 16)), jnp.float32)
    integrals = scatter_about(key_of[1], (NV, NV, SLAB, NV), (NV * NV // 8) ** -0.5, 0.03125, ((0, 16), (1, 16)), jnp.float32)
    virt_irrep = touch_ends(skewed_ids(key_of[2], (NV,), 8, 2), jax.random.fold_in(key_of[2], 3), 0, 7).astype(jnp.int32)
    occ_irrep = touch_ends(jax.random.randint(key_of[3], (NO,), 0, 8), jax.random.fold_in(key_of[3], 1), 0, 7).astype(jnp.int32)
    pair_index = touch_ends(jax.random.randint(key_of[4], (PAIRS, 2), 0, NO), jax.random.fold_in(key_of[4], 1), 0, NO - 1).astype(jnp.int32)
    return dict(amplitudes=amplitudes, integrals=integrals, virt_irrep=virt_irrep, occ_irrep=occ_irrep, pair_index=pair_index)


def reference(amplitudes, integrals, virt_irrep, occ_irrep, pair_index):
    pair_sym = jnp.bitwise_xor(occ_irrep[pair_index[:, 0]], occ_irrep[pair_index[:, 1]])
    cd_sym = jnp.bitwise_xor(virt_irrep[:, None], virt_irrep[None, :])
    amp_sym = jnp.where(cd_sym[None, :, :] == pair_sym[:, None, None], amplitudes, jnp.float32(0.0))
    ladder_full = jnp.dot(amp_sym.reshape(PAIRS, NV * NV), integrals.reshape(NV * NV, SLAB * NV),
                          precision=lax.Precision.HIGHEST, preferred_element_type=jnp.float32)
    ladder_full = ladder_full.reshape(PAIRS, SLAB, NV)
    ab_sym = jnp.bitwise_xor(virt_irrep[:SLAB][:, None], virt_irrep[None, :])
    keep = ab_sym[None, :, :] == pair_sym[:, None, None]
    return jnp.where(keep, ladder_full, jnp.float32(0.0))
```

```python
import functools

import jax
import jax.numpy as jnp
from jax import lax
from jax.experimental import pallas as pl
from jax.experimental.pallas import tpu as pltpu
from jax.sharding import Mesh, PartitionSpec as P

F32 = jnp.float32
BF16 = jnp.bfloat16
I32 = jnp.int32

C = 36
D = 36
PD = 32
NY = NX = 4
NR = NY * NX
NZ = 8
SLAB = 3
NV = 576
PAIRS = 512
NO = 60
CP = 40
K = D * CP
KP = 1536
FITS = ((6, 1), (6, 2), (9, 3))

SMEM = pl.BlockSpec(memory_space=pltpu.SMEM)
VMEM = pl.BlockSpec(memory_space=pltpu.VMEM)
HBM = pl.BlockSpec(memory_space=pltpu.HBM)


def rows_of(slots):
    return -(-slots * 36 // 8) * 8


def in_hbm(x):
    return pltpu.with_memory_space_constraint(x, pltpu.HBM)


def labels_kernel(occ_ref, virt_ref, pairs_ref, row_ref, sym_ref, slot_ref, which_ref):
    pairs = pairs_ref[...]
    found = jnp.zeros_like(pairs)
    for o in range(NO):
        found = jnp.where(pairs == o, occ_ref[o], found)
    sym_ref[...] = jnp.bitwise_xor(found[0:1], found[1:2])

    labels = row_ref[...]
    at = lax.rem(lax.broadcasted_iota(I32, labels.shape, 1), D)
    place = jnp.zeros_like(labels)
    for k in range(1, D):
        same = (pltpu.roll(labels, k, 1) == labels) & (at >= k)
        place = place + same.astype(I32)
    top = jnp.max(place)
    deep = jnp.maximum(slab_slot(virt_ref, jnp.int32(1)), slab_slot(virt_ref, jnp.int32(2)))
    which = jnp.int32(len(FITS) - 1)
    for i, (tiles, slots) in reversed(list(enumerate(FITS[:-1]))):
        which = jnp.where((top < 4 * tiles) & (deep < slots), i, which)
    which_ref[0] = which
    slot_ref[...] = jnp.where(which < len(FITS) - 1, place, at)


def slab_slot(virt_ref, a):
    first = (a > 0) & (virt_ref[0] == virt_ref[a])
    second = (a > 1) & (virt_ref[1] == virt_ref[a])
    return first.astype(I32) + second.astype(I32)


def label_all(occ_irrep, virt_irrep, pairs, virt_row):
    return pl.pallas_call(
        labels_kernel,
        out_shape=[
            jax.ShapeDtypeStruct((1, PAIRS), I32),
            jax.ShapeDtypeStruct((1, NV), I32),
            jax.ShapeDtypeStruct((1,), I32),
        ],
        in_specs=[SMEM, SMEM, VMEM, VMEM],
        out_specs=[VMEM, VMEM, SMEM],
        name="label_all",
    )(occ_irrep, virt_irrep, pairs, virt_row)


def pack_kernel(tiles, at_ref, virt_ref, slot_ref, x_hbm, cl_ref, sym_ref, o_hbm, x_buf, f_buf, t_buf, o_buf, in_sems, out_sems):
    def fetch(q):
        return pltpu.make_async_copy(x_hbm.at[pl.ds(4 * q, 4)], x_buf.at[pl.ds(4 * q, 4)], in_sems.at[q])

    for q in range(D // 4):
        fetch(q).start()
    f_buf[...] = jnp.zeros_like(f_buf)
    pair = at_ref[0] * PD + lax.broadcasted_iota(I32, (PD, PAIRS), 0)
    mine = lax.broadcasted_iota(I32, (PD, PAIRS), 1) == pair
    sym = jnp.sum(jnp.where(mine, sym_ref[...], 0), axis=1, keepdims=True)
    first = at_ref[1] * D

    @pl.loop(0, D // 4)
    def _(q):
        fetch(q).wait()
        for i in range(4):
            d = 4 * q + i
            keep = jnp.bitwise_xor(cl_ref[...], virt_ref[first + d]) == sym
            at = slot_ref[0, first + d]
            f_buf[at] = f_buf[at] + jnp.where(keep, x_buf[d], 0.0)

    for q in range(tiles):
        t_buf[q % 2] = f_buf[4 * q:4 * q + 4].reshape(4 * PD, NV).T
        for r in range(NR):
            o_buf[r, q * C:(q + 1) * C, :] = t_buf[q % 2, r * C:(r + 1) * C, :]
    out = []
    for r in range(NR):
        copy = pltpu.make_async_copy(o_buf.at[r], o_hbm.at[r], out_sems.at[r])
        copy.start()
        out.append(copy)
    for copy in out:
        copy.wait()


def pack_amplitudes(tiles, at, virt, slots, amps, cl, sym):
    block = (NR, tiles * C, 128)
    return pl.pallas_call(
        functools.partial(pack_kernel, tiles),
        out_shape=pltpu.HBM(block, F32),
        in_specs=[SMEM, SMEM, SMEM, HBM, VMEM, VMEM],
        out_specs=HBM,
        scratch_shapes=[
            pltpu.VMEM((D, PD, NV), F32),
            pltpu.VMEM((4 * tiles, PD, NV), F32),
            pltpu.VMEM((2, NV, 128), F32),
            pltpu.VMEM(block, F32),
            pltpu.SemaphoreType.DMA((D // 4,)),
            pltpu.SemaphoreType.DMA((NR,)),
        ],
        compiler_params=pltpu.CompilerParams(vmem_limit_bytes=20 << 20),
        name="pack_amplitudes",
    )(at, virt, slots, in_hbm(amps), cl, sym)


STEP = 6


def integrals_kernel(v_hbm, hi_hbm, lo_hbm, v_buf, h_buf, l_buf, in_sems, out_sems):
    def fetch(d, a):
        return pltpu.make_async_copy(v_hbm.at[:, a, d], v_buf.at[d, a], in_sems.at[d, a])

    @pl.loop(0, D)
    def _(d):
        for a in range(SLAB):
            fetch(d, a).start()

    zero = jnp.zeros((CP - C, NV), F32)
    for a in range(SLAB):
        h_buf[a, K:, :] = jnp.zeros((KP - K, NV), BF16)
        l_buf[a, K:, :] = jnp.zeros((KP - K, NV), BF16)
    out = []
    for i in range(D // STEP):
        @pl.loop(i * STEP // 2, (i + 1) * STEP // 2)
        def _(pair):
            d = 2 * pair
            at = pl.multiple_of(pair * 2 * CP, 16)
            for a in range(SLAB):
                fetch(d, a).wait()
                fetch(d + 1, a).wait()
                x = jnp.concatenate([v_buf[d, a], zero, v_buf[d + 1, a], zero], axis=0)
                h = x.astype(BF16)
                h_buf[a, pl.ds(at, 2 * CP), :] = h
                l_buf[a, pl.ds(at, 2 * CP), :] = (x - h.astype(F32)).astype(BF16)

        rows = pl.ds(i * STEP * CP, STEP * CP if (i + 1) * STEP < D else KP - i * STEP * CP)
        for n, (buf, hbm) in enumerate(((h_buf, hi_hbm), (l_buf, lo_hbm))):
            copy = pltpu.make_async_copy(buf.at[:, rows], hbm.at[:, rows], out_sems.at[n, i])
            copy.start()
            out.append(copy)
    for copy in out:
        copy.wait()


def split_integrals(v_t):
    block = (SLAB, KP, NV)
    return pl.pallas_call(
        integrals_kernel,
        out_shape=[pltpu.HBM(block, BF16)] * 2,
        in_specs=[HBM],
        out_specs=[HBM] * 2,
        scratch_shapes=[
            pltpu.VMEM((D, SLAB, C, NV), F32),
            pltpu.VMEM(block, BF16),
            pltpu.VMEM(block, BF16),
            pltpu.SemaphoreType.DMA((D, SLAB)),
            pltpu.SemaphoreType.DMA((2, D // STEP)),
        ],
        compiler_params=pltpu.CompilerParams(vmem_limit_bytes=28 << 20),
        cost_estimate=pl.CostEstimate(flops=20_000_000, bytes_accessed=36_000_000, transcendentals=0),
        name="split_integrals",
    )(in_hbm(v_t))


def regroup(blocks):
    lane = lax.broadcasted_iota(I32, blocks[0].shape, 1) // 32
    out = []
    for i in range(4):
        total = None
        for s in range(4):
            piece = blocks[s] if s == i else pltpu.roll(blocks[s], (32 * (s - i)) % 128, 1)
            total = piece if total is None else jnp.where(lane == s, piece, total)
        out.append(total)
    return out


def tn_dot(x, y):
    return lax.dot_general(x, y, (((0,), (0,)), ((), ())), preferred_element_type=F32)


def products_kernel(slots, at_ref, virt_ref, slot_ref, r_ref, sym_ref, cl_ref, bl_ref, vh_hbm, vl_hbm,
                    own_ref, away_ref, f_buf, h_buf, l_buf, t_buf, vh_ref, vl_ref, sems):
    def fetch(a, n):
        hbm, buf = ((vh_hbm, vh_ref), (vl_hbm, vl_ref))[n]
        return pltpu.make_async_copy(hbm.at[a], buf.at[a], sems.at[a, n])

    for a in range(SLAB):
        for n in range(2):
            fetch(a, n).start()
    first = at_ref[1] * D
    h_buf[K:, :] = jnp.zeros((KP - K, PAIRS), BF16)
    l_buf[K:, :] = jnp.zeros((KP - K, PAIRS), BF16)
    zero = jnp.zeros((CP - C, 128), F32)
    tiles = r_ref.shape[1] // C

    @pl.loop(0, NY)
    def _(y):
        for q in range(tiles):
            blocks = [jnp.concatenate([r_ref[4 * y + s, q * C:(q + 1) * C, :], zero], axis=0) for s in range(4)]
            for i, x in enumerate(regroup(blocks)):
                f_buf[y, 4 * q + i] = x

    @pl.loop(0, D // 2)
    def _(pair):
        d = 2 * pair
        at = pl.multiple_of(pair * 2 * CP, 16)
        for y in range(NY):
            cut = slice(y * 128, (y + 1) * 128)
            labels = jnp.bitwise_xor(cl_ref[...], sym_ref[:, cut])
            parts = [jnp.where(labels == virt_ref[first + e], f_buf[y, slot_ref[0, first + e]], 0.0) for e in (d, d + 1)]
            x = jnp.concatenate(parts, axis=0)
            h = x.astype(BF16)
            h_buf[pl.ds(at, 2 * CP), cut] = h
            l_buf[pl.ds(at, 2 * CP), cut] = (x - h.astype(F32)).astype(BF16)

    if slots < SLAB:
        t_buf[...] = jnp.zeros_like(t_buf)

    @pl.loop(0, SLAB)
    def _(a):
        fetch(a, 0).wait()
        fetch(a, 1).wait()
        out = tn_dot(vh_ref[a], h_buf[...])
        out += tn_dot(vh_ref[a], l_buf[...])
        out += tn_dot(vl_ref[a], h_buf[...])
        if slots < SLAB:
            at = slab_slot(virt_ref, a)
            for y in range(NY):
                cut = slice(y * 128, (y + 1) * 128)
                keep = jnp.bitwise_xor(bl_ref[...], virt_ref[a]) == sym_ref[:, cut]
                t_buf[at, :, cut] = t_buf[at, :, cut] + jnp.where(keep, out[:, cut], 0.0)
        else:
            t_buf[a] = out

    for flag in range(2):
        @pl.when(at_ref[2] == flag)
        def _():
            for j in range(2 * NZ):
                o_ref = own_ref if j % 2 == flag else away_ref
                for t in range(slots):
                    o_ref[j // 2, t * 36:(t + 1) * 36, :] = t_buf[t, j * 36:(j + 1) * 36, :]
    tail = rows_of(slots) - slots * 36
    if tail:
        for z in range(NZ):
            own_ref[z, slots * 36:, :] = jnp.zeros((tail, PAIRS), F32)
            away_ref[z, slots * 36:, :] = jnp.zeros((tail, PAIRS), F32)


def products(slots, at, virt, dslots, recv, sym, cl, bl, vh, vl):
    block = jax.ShapeDtypeStruct((NZ, rows_of(slots), PAIRS), F32)
    folded = recv.shape[1] // C * 4
    return pl.pallas_call(
        functools.partial(products_kernel, slots),
        out_shape=[block, block],
        in_specs=[SMEM] * 3 + [VMEM] * 4 + [HBM] * 2,
        out_specs=[VMEM] * 2,
        scratch_shapes=[
            pltpu.VMEM((NY, folded, CP, 128), F32),
            pltpu.VMEM((KP, PAIRS), BF16),
            pltpu.VMEM((KP, PAIRS), BF16),
            pltpu.VMEM((slots, NV, PAIRS), F32),
            pltpu.VMEM((SLAB, KP, NV), BF16),
            pltpu.VMEM((SLAB, KP, NV), BF16),
            pltpu.SemaphoreType.DMA((SLAB, 2)),
        ],
        compiler_params=pltpu.CompilerParams(vmem_limit_bytes=34 << 20),
        cost_estimate=pl.CostEstimate(flops=2 * 3 * NV * SLAB * KP * PAIRS, bytes_accessed=10_000_000, transcendentals=0),
        name="products",
    )(at, virt, dslots, recv, sym, cl, bl, in_hbm(vh), in_hbm(vl))


def pair_kernel(slots, own_ref, other_ref, o_hbm, o_buf, sems):
    jb = rows_of(slots)

    def put(r):
        return pltpu.make_async_copy(o_buf.at[r], o_hbm.at[r], sems.at[r])

    for y in range(NY):
        cut = slice(y * 128, (y + 1) * 128)
        for h in range(2):
            blocks = [own_ref[2 * rb + h, :, cut] + other_ref[2 * rb + h, :, cut] for rb in range(4)]
            for x, block in enumerate(regroup(blocks)):
                o_buf[4 * y + x, h * jb:(h + 1) * jb, :] = block
        for x in range(NX):
            put(4 * y + x).start()
    for r in range(NR):
        put(r).wait()


def sum_pair(slots, own, other):
    block = (NR, 2 * rows_of(slots), 128)
    return pl.pallas_call(
        functools.partial(pair_kernel, slots),
        out_shape=pltpu.HBM(block, F32),
        in_specs=[VMEM] * 2,
        out_specs=HBM,
        scratch_shapes=[pltpu.VMEM(block, F32), pltpu.SemaphoreType.DMA((NR,))],
        compiler_params=pltpu.CompilerParams(vmem_limit_bytes=8 << 20),
        name="sum_pair",
    )(own, other)


def row_kernel(slots, x_ref, o_ref):
    jb = rows_of(slots)
    total = x_ref[0]
    for s in range(1, NR):
        total = total + x_ref[s]
    zero = jnp.zeros((128 - jb, 128), F32)
    for h in range(2):
        turned = jnp.concatenate([total[h * jb:(h + 1) * jb, :], zero], axis=0).T
        for rb in range(4):
            o_ref[2 * rb + h] = turned[rb * 32:(rb + 1) * 32, :]


def sum_row(slots, x):
    return pl.pallas_call(
        functools.partial(row_kernel, slots),
        out_shape=jax.ShapeDtypeStruct((NZ, PD, 128), F32),
        in_specs=[VMEM],
        out_specs=VMEM,
        compiler_params=pltpu.CompilerParams(vmem_limit_bytes=8 << 20),
        name="sum_row",
    )(x)


def last_kernel(slots, virt_ref, x_ref, sym_ref, lab_ref, o_ref):
    total = x_ref[0]
    for s in range(1, NZ):
        total = total + x_ref[s]
    for a in range(SLAB):
        at = slab_slot(virt_ref, jnp.int32(a)) if slots < SLAB else jnp.int32(a)
        x = pltpu.roll(total, lax.rem(128 - 36 * at, 128), 1) if slots > 1 else total
        keep = jnp.bitwise_xor(lab_ref[...], virt_ref[a]) == sym_ref[:, 0:36]
        o_ref[a] = jnp.where(keep, x[:, 0:36], 0.0)


def sum_last(slots, virt, x, sym, lab):
    return pl.pallas_call(
        functools.partial(last_kernel, slots),
        out_shape=jax.ShapeDtypeStruct((SLAB, PD, 36), F32),
        in_specs=[SMEM] + [VMEM] * 3,
        out_specs=VMEM,
        name="sum_last",
    )(virt, x, sym, lab)


def ladder(tiles, slots, amps_t, v_t, virt, virt_row, sym, dslots, at):
    labels_c = lax.dynamic_slice_in_dim(virt, at[0] * C, C)
    labels_d = lax.dynamic_slice_in_dim(virt, at[1] * D, D)
    cl = jnp.broadcast_to(jnp.pad(labels_c, (0, CP - C))[:, None], (CP, 128))
    bl = jnp.broadcast_to(virt[:, None], (NV, 128))
    local_sym = lax.dynamic_slice_in_dim(sym[0], at[0] * PD, PD)
    local_sym = jnp.broadcast_to(local_sym[:, None], (PD, 128))

    sent = pack_amplitudes(tiles, at, virt, dslots, amps_t, virt_row, sym)
    recv = lax.all_to_all(sent, ("y", "x"), 0, 0, tiled=True)
    vh, vl = split_integrals(v_t)
    own, away = products(slots, at, virt, dslots, recv, sym, cl, bl, vh, vl)
    other = lax.ppermute(away, "core", [(0, 1), (1, 0)])
    by_row = lax.all_to_all(sum_pair(slots, own, other), ("y", "x"), 0, 0, tiled=True)
    by_z = lax.all_to_all(sum_row(slots, by_row), "z", 0, 0, tiled=True)
    return sum_last(slots, virt, by_z, local_sym, labels_d.reshape(1, D))


def per_device(amplitudes, integrals, virt_irrep, occ_irrep, pair_index):
    row_at = lax.axis_index("y") * NX + lax.axis_index("x")
    core_at = lax.axis_index("core")
    at = jnp.stack([row_at, lax.axis_index("z") * 2 + core_at, core_at]).astype(I32)
    amps_t = jnp.transpose(amplitudes, (2, 0, 1))
    v_t = jnp.transpose(integrals, (0, 2, 1, 3))
    virt_row = virt_irrep.reshape(1, NV)
    sym, dslots, which = label_all(occ_irrep, virt_irrep, pair_index.T, virt_row)
    programs = [functools.partial(ladder, tiles, slots) for tiles, slots in FITS]
    out = lax.switch(which[0], programs, amps_t, v_t, virt_irrep, virt_row, sym, dslots, at)
    return jnp.transpose(out, (1, 0, 2))


def solution(mesh):
    fine = Mesh(mesh.devices.reshape(NY, NX, NZ, 2), ("y", "x", "z", "core"))
    rows, cols = ("y", "x"), ("z", "core")
    return jax.shard_map(
        per_device,
        mesh=fine,
        in_specs=(P(rows, None, cols), P(rows, cols, None, None), P(), P(), P()),
        out_specs=P(rows, None, cols),
        check_vma=False,
    )
```

```python
import functools

import jax
import jax.numpy as jnp
from jax import lax
from jax.experimental import pallas as pl
from jax.experimental.pallas import tpu as pltpu
from jax.sharding import Mesh, PartitionSpec as P

F32 = jnp.float32
BF16 = jnp.bfloat16
I32 = jnp.int32

C = 36
D = 36
PD = 32
NY = NX = 4
NR = NY * NX
NZ = 8
SLAB = 3
NV = 576
PAIRS = 512
NO = 60
CP = 40
K = D * CP
KP = 1536
FITS = ((5, 1), (5, 2), (6, 2), (9, 3))

SMEM = pl.BlockSpec(memory_space=pltpu.SMEM)
VMEM = pl.BlockSpec(memory_space=pltpu.VMEM)
HBM = pl.BlockSpec(memory_space=pltpu.HBM)


def rows_of(slots):
    return -(-slots * 36 // 8) * 8


def in_hbm(x):
    return pltpu.with_memory_space_constraint(x, pltpu.HBM)


def labels_kernel(occ_ref, virt_ref, pairs_ref, row_ref, sym_ref, slot_ref, which_ref):
    pairs = pairs_ref[...]
    found = jnp.zeros_like(pairs)
    for o in range(NO):
        found = jnp.where(pairs == o, occ_ref[o], found)
    sym_ref[...] = jnp.bitwise_xor(found[0:1], found[1:2])

    labels = jnp.concatenate([row_ref[...], row_ref[:, 0:64]], axis=1)
    lane = lax.broadcasted_iota(I32, labels.shape, 1)
    at = lax.rem(lane, D)
    place = jnp.zeros_like(labels)
    for k in range(1, D):
        same = pltpu.roll(labels, k, 1) == labels
        place = place + (same & (at >= k)).astype(I32)
    top = jnp.max(jnp.where(lane < NV, place, 0))
    deep = jnp.maximum(slab_slot(virt_ref, jnp.int32(1)), slab_slot(virt_ref, jnp.int32(2)))
    which = jnp.int32(len(FITS) - 1)
    for i, (tiles, slots) in reversed(list(enumerate(FITS[:-1]))):
        which = jnp.where((top < 4 * tiles) & (deep < slots), i, which)
    which_ref[0] = which
    slot_ref[...] = jnp.where(which < len(FITS) - 1, place, at)[:, 0:NV]


def slab_slot(virt_ref, a):
    first = (a > 0) & (virt_ref[0] == virt_ref[a])
    second = (a > 1) & (virt_ref[1] == virt_ref[a])
    return first.astype(I32) + second.astype(I32)


def label_all(occ_irrep, virt_irrep, pairs, virt_row):
    return pl.pallas_call(
        labels_kernel,
        out_shape=[
            jax.ShapeDtypeStruct((1, PAIRS), I32),
            jax.ShapeDtypeStruct((1, NV), I32),
            jax.ShapeDtypeStruct((1,), I32),
        ],
        in_specs=[SMEM, SMEM, VMEM, VMEM],
        out_specs=[VMEM, VMEM, SMEM],
        name="label_all",
    )(occ_irrep, virt_irrep, pairs, virt_row)


def own_column(at_ref, sym_ref):
    pair = at_ref[0] * PD + lax.broadcasted_iota(I32, (PD, PAIRS), 0)
    mine = lax.broadcasted_iota(I32, (PD, PAIRS), 1) == pair
    return jnp.sum(jnp.where(mine, sym_ref[...], 0), axis=1, keepdims=True)


def pack_kernel(tiles, at_ref, virt_ref, slot_ref, x_hbm, cl_ref, sym_ref, o_hbm, x_buf, f_buf, t_buf, o_buf, in_sems, out_sems):
    def fetch(q):
        return pltpu.make_async_copy(x_hbm.at[pl.ds(4 * q, 4)], x_buf.at[pl.ds(4 * q, 4)], in_sems.at[q])

    for q in range(D // 4):
        fetch(q).start()
    f_buf[...] = jnp.zeros_like(f_buf)
    sym = own_column(at_ref, sym_ref)
    first = at_ref[1] * D

    @pl.loop(0, D // 4)
    def _(q):
        fetch(q).wait()
        for i in range(4):
            d = 4 * q + i
            keep = jnp.bitwise_xor(cl_ref[...], virt_ref[first + d]) == sym
            at = slot_ref[0, first + d]
            f_buf[at] = f_buf[at] + jnp.where(keep, x_buf[d], 0.0)

    for q in range(tiles):
        t_buf[q % 2] = f_buf[4 * q:4 * q + 4].reshape(4 * PD, NV).T
        for r in range(NR):
            o_buf[r, q * C:(q + 1) * C, :] = t_buf[q % 2, r * C:(r + 1) * C, :]
    out = []
    for r in range(NR):
        copy = pltpu.make_async_copy(o_buf.at[r], o_hbm.at[r], out_sems.at[r])
        copy.start()
        out.append(copy)
    for copy in out:
        copy.wait()


def pack_amplitudes(tiles, at, virt, slots, amps, cl, sym):
    block = (NR, tiles * C, 128)
    return pl.pallas_call(
        functools.partial(pack_kernel, tiles),
        out_shape=pltpu.HBM(block, F32),
        in_specs=[SMEM, SMEM, SMEM, HBM, VMEM, VMEM],
        out_specs=HBM,
        scratch_shapes=[
            pltpu.VMEM((D, PD, NV), F32),
            pltpu.VMEM((4 * tiles, PD, NV), F32),
            pltpu.VMEM((2, NV, 128), F32),
            pltpu.VMEM(block, F32),
            pltpu.SemaphoreType.DMA((D // 4,)),
            pltpu.SemaphoreType.DMA((NR,)),
        ],
        compiler_params=pltpu.CompilerParams(vmem_limit_bytes=20 << 20),
        name="pack_amplitudes",
    )(at, virt, slots, in_hbm(amps), cl, sym)


STEP = 6


def integrals_kernel(v_hbm, hi_hbm, lo_hbm, v_buf, h_buf, l_buf, in_sems, out_sems):
    def fetch(d, a):
        return pltpu.make_async_copy(v_hbm.at[:, a, d], v_buf.at[d, a], in_sems.at[d, a])

    @pl.loop(0, D)
    def _(d):
        for a in range(SLAB):
            fetch(d, a).start()

    zero = jnp.zeros((CP - C, NV), F32)
    for a in range(SLAB):
        h_buf[a, K:, :] = jnp.zeros((KP - K, NV), BF16)
        l_buf[a, K:, :] = jnp.zeros((KP - K, NV), BF16)
    out = []
    for i in range(D // STEP):
        @pl.loop(i * STEP // 2, (i + 1) * STEP // 2)
        def _(pair):
            d = 2 * pair
            at = pl.multiple_of(pair * 2 * CP, 16)
            for a in range(SLAB):
                fetch(d, a).wait()
                fetch(d + 1, a).wait()
                x = jnp.concatenate([v_buf[d, a], zero, v_buf[d + 1, a], zero], axis=0)
                h = x.astype(BF16)
                h_buf[a, pl.ds(at, 2 * CP), :] = h
                l_buf[a, pl.ds(at, 2 * CP), :] = (x - h.astype(F32)).astype(BF16)

        rows = pl.ds(i * STEP * CP, STEP * CP if (i + 1) * STEP < D else KP - i * STEP * CP)
        for n, (buf, hbm) in enumerate(((h_buf, hi_hbm), (l_buf, lo_hbm))):
            copy = pltpu.make_async_copy(buf.at[:, rows], hbm.at[:, rows], out_sems.at[n, i])
            copy.start()
            out.append(copy)
    for copy in out:
        copy.wait()


def split_integrals(v_t):
    block = (SLAB, KP, NV)
    return pl.pallas_call(
        integrals_kernel,
        out_shape=[pltpu.HBM(block, BF16)] * 2,
        in_specs=[HBM],
        out_specs=[HBM] * 2,
        scratch_shapes=[
            pltpu.VMEM((D, SLAB, C, NV), F32),
            pltpu.VMEM(block, BF16),
            pltpu.VMEM(block, BF16),
            pltpu.SemaphoreType.DMA((D, SLAB)),
            pltpu.SemaphoreType.DMA((2, D // STEP)),
        ],
        compiler_params=pltpu.CompilerParams(vmem_limit_bytes=28 << 20),
        cost_estimate=pl.CostEstimate(flops=20_000_000, bytes_accessed=36_000_000, transcendentals=0),
        name="split_integrals",
    )(in_hbm(v_t))


def regroup(blocks):
    lane = lax.broadcasted_iota(I32, blocks[0].shape, 1) // 32
    out = []
    for i in range(4):
        total = None
        for s in range(4):
            piece = blocks[s] if s == i else pltpu.roll(blocks[s], (32 * (s - i)) % 128, 1)
            total = piece if total is None else jnp.where(lane == s, piece, total)
        out.append(total)
    return out


def tn_dot(x, y):
    return lax.dot_general(x, y, (((0,), (0,)), ((), ())), preferred_element_type=F32)


def products_kernel(slots, at_ref, virt_ref, slot_ref, r_ref, sym_ref, cl_ref, bl_ref, vh_hbm, vl_hbm,
                    own_ref, away_ref, f_buf, h_buf, l_buf, t_buf, vh_ref, vl_ref, sems):
    def fetch(a, n):
        hbm, buf = ((vh_hbm, vh_ref), (vl_hbm, vl_ref))[n]
        return pltpu.make_async_copy(hbm.at[a], buf.at[a], sems.at[a, n])

    for a in range(SLAB):
        for n in range(2):
            fetch(a, n).start()
    first = at_ref[1] * D
    h_buf[K:, :] = jnp.zeros((KP - K, PAIRS), BF16)
    l_buf[K:, :] = jnp.zeros((KP - K, PAIRS), BF16)
    zero = jnp.zeros((CP - C, 128), F32)
    tiles = r_ref.shape[1] // C

    @pl.loop(0, NY)
    def _(y):
        for q in range(tiles):
            blocks = [jnp.concatenate([r_ref[4 * y + s, q * C:(q + 1) * C, :], zero], axis=0) for s in range(4)]
            for i, x in enumerate(regroup(blocks)):
                f_buf[y, 4 * q + i] = x

    @pl.loop(0, D // 2)
    def _(pair):
        d = 2 * pair
        at = pl.multiple_of(pair * 2 * CP, 16)
        for y in range(NY):
            cut = slice(y * 128, (y + 1) * 128)
            labels = jnp.bitwise_xor(cl_ref[...], sym_ref[:, cut])
            parts = [jnp.where(labels == virt_ref[first + e], f_buf[y, slot_ref[0, first + e]], 0.0) for e in (d, d + 1)]
            x = jnp.concatenate(parts, axis=0)
            h = x.astype(BF16)
            h_buf[pl.ds(at, 2 * CP), cut] = h
            l_buf[pl.ds(at, 2 * CP), cut] = (x - h.astype(F32)).astype(BF16)

    if slots < SLAB:
        t_buf[...] = jnp.zeros_like(t_buf)

    @pl.loop(0, SLAB)
    def _(a):
        fetch(a, 0).wait()
        fetch(a, 1).wait()
        out = tn_dot(vh_ref[a], h_buf[...])
        out += tn_dot(vh_ref[a], l_buf[...])
        out += tn_dot(vl_ref[a], h_buf[...])
        if slots < SLAB:
            at = slab_slot(virt_ref, a)
            for y in range(NY):
                cut = slice(y * 128, (y + 1) * 128)
                keep = jnp.bitwise_xor(bl_ref[...], virt_ref[a]) == sym_ref[:, cut]
                t_buf[at, :, cut] = t_buf[at, :, cut] + jnp.where(keep, out[:, cut], 0.0)
        else:
            t_buf[a] = out

    for flag in range(2):
        @pl.when(at_ref[2] == flag)
        def _():
            for j in range(2 * NZ):
                o_ref = own_ref if j % 2 == flag else away_ref
                for t in range(slots):
                    o_ref[j // 2, t * 36:(t + 1) * 36, :] = t_buf[t, j * 36:(j + 1) * 36, :]
    tail = rows_of(slots) - slots * 36
    if tail:
        for z in range(NZ):
            own_ref[z, slots * 36:, :] = jnp.zeros((tail, PAIRS), F32)
            away_ref[z, slots * 36:, :] = jnp.zeros((tail, PAIRS), F32)


def products(slots, at, virt, dslots, recv, sym, cl, bl, vh, vl):
    block = jax.ShapeDtypeStruct((NZ, rows_of(slots), PAIRS), F32)
    folded = recv.shape[1] // C * 4
    return pl.pallas_call(
        functools.partial(products_kernel, slots),
        out_shape=[block, block],
        in_specs=[SMEM] * 3 + [VMEM] * 4 + [HBM] * 2,
        out_specs=[VMEM] * 2,
        scratch_shapes=[
            pltpu.VMEM((NY, folded, CP, 128), F32),
            pltpu.VMEM((KP, PAIRS), BF16),
            pltpu.VMEM((KP, PAIRS), BF16),
            pltpu.VMEM((slots, NV, PAIRS), F32),
            pltpu.VMEM((SLAB, KP, NV), BF16),
            pltpu.VMEM((SLAB, KP, NV), BF16),
            pltpu.SemaphoreType.DMA((SLAB, 2)),
        ],
        compiler_params=pltpu.CompilerParams(vmem_limit_bytes=34 << 20),
        cost_estimate=pl.CostEstimate(flops=2 * 3 * NV * SLAB * KP * PAIRS, bytes_accessed=10_000_000, transcendentals=0),
        name="products",
    )(at, virt, dslots, recv, sym, cl, bl, in_hbm(vh), in_hbm(vl))


def pair_kernel(slots, own_ref, other_ref, o_hbm, o_buf, sems):
    jb = rows_of(slots)

    def put(r):
        return pltpu.make_async_copy(o_buf.at[r], o_hbm.at[r], sems.at[r])

    for y in range(NY):
        cut = slice(y * 128, (y + 1) * 128)
        for h in range(2):
            blocks = [own_ref[2 * rb + h, :, cut] + other_ref[2 * rb + h, :, cut] for rb in range(4)]
            for x, block in enumerate(regroup(blocks)):
                o_buf[4 * y + x, h * jb:(h + 1) * jb, :] = block
        for x in range(NX):
            put(4 * y + x).start()
    for r in range(NR):
        put(r).wait()


def sum_pair(slots, own, other):
    block = (NR, 2 * rows_of(slots), 128)
    return pl.pallas_call(
        functools.partial(pair_kernel, slots),
        out_shape=pltpu.HBM(block, F32),
        in_specs=[VMEM] * 2,
        out_specs=HBM,
        scratch_shapes=[pltpu.VMEM(block, F32), pltpu.SemaphoreType.DMA((NR,))],
        compiler_params=pltpu.CompilerParams(vmem_limit_bytes=8 << 20),
        name="sum_pair",
    )(own, other)


def row_kernel(slots, x_ref, o_ref):
    jb = rows_of(slots)
    total = x_ref[0]
    for s in range(1, NR):
        total = total + x_ref[s]
    zero = jnp.zeros((128 - jb, 128), F32)
    for h in range(2):
        turned = jnp.concatenate([total[h * jb:(h + 1) * jb, :], zero], axis=0).T
        for rb in range(4):
            o_ref[2 * rb + h] = turned[rb * 32:(rb + 1) * 32, :]


def sum_row(slots, x):
    return pl.pallas_call(
        functools.partial(row_kernel, slots),
        out_shape=jax.ShapeDtypeStruct((NZ, PD, 128), F32),
        in_specs=[VMEM],
        out_specs=VMEM,
        compiler_params=pltpu.CompilerParams(vmem_limit_bytes=8 << 20),
        name="sum_row",
    )(x)


def last_kernel(slots, at_ref, virt_ref, x_ref, sym_ref, lab_ref, o_ref):
    total = x_ref[0]
    for s in range(1, NZ):
        total = total + x_ref[s]
    sym = own_column(at_ref, sym_ref)
    for a in range(SLAB):
        at = slab_slot(virt_ref, jnp.int32(a)) if slots < SLAB else a
        x = total[:, 0:36]
        for t in range(1, slots):
            x = jnp.where(at == t, total[:, t * 36:(t + 1) * 36], x)
        keep = jnp.bitwise_xor(lab_ref[...], virt_ref[a]) == sym
        o_ref[a] = jnp.where(keep, x, 0.0)


def sum_last(slots, at, virt, x, sym, lab):
    return pl.pallas_call(
        functools.partial(last_kernel, slots),
        out_shape=jax.ShapeDtypeStruct((SLAB, PD, 36), F32),
        in_specs=[SMEM] * 2 + [VMEM] * 3,
        out_specs=VMEM,
        compiler_params=pltpu.CompilerParams(vmem_limit_bytes=8 << 20),
        name="sum_last",
    )(at, virt, x, sym, lab)


def ladder(tiles, slots, amps_t, v_t, virt, virt_row, sym, dslots, at):
    labels_c = lax.dynamic_slice_in_dim(virt, at[0] * C, C)
    lab = lax.dynamic_slice_in_dim(virt, at[1] * D, D).reshape(1, D)
    cl = jnp.broadcast_to(jnp.pad(labels_c, (0, CP - C))[:, None], (CP, 128))
    bl = jnp.broadcast_to(virt[:, None], (NV, 128))

    sent = pack_amplitudes(tiles, at, virt, dslots, amps_t, virt_row, sym)
    recv = lax.all_to_all(sent, ("y", "x"), 0, 0, tiled=True)
    vh, vl = split_integrals(v_t)
    own, away = products(slots, at, virt, dslots, recv, sym, cl, bl, vh, vl)
    other = lax.ppermute(away, "core", [(0, 1), (1, 0)])
    by_row = lax.all_to_all(sum_pair(slots, own, other), ("y", "x"), 0, 0, tiled=True)
    by_z = lax.all_to_all(sum_row(slots, by_row), "z", 0, 0, tiled=True)
    return sum_last(slots, at, virt, by_z, sym, lab)


def per_device(amplitudes, integrals, virt_irrep, occ_irrep, pair_index):
    row_at = lax.axis_index("y") * NX + lax.axis_index("x")
    core_at = lax.axis_index("core")
    at = jnp.stack([row_at, lax.axis_index("z") * 2 + core_at, core_at]).astype(I32)
    amps_t = jnp.transpose(amplitudes, (2, 0, 1))
    v_t = jnp.transpose(integrals, (0, 2, 1, 3))
    virt_row = virt_irrep.reshape(1, NV)
    sym, dslots, which = label_all(occ_irrep, virt_irrep, pair_index.T, virt_row)
    programs = [functools.partial(ladder, tiles, slots) for tiles, slots in FITS]
    out = lax.switch(which[0], programs, amps_t, v_t, virt_irrep, virt_row, sym, dslots, at)
    return jnp.transpose(out, (1, 0, 2))


def solution(mesh):
    fine = Mesh(mesh.devices.reshape(NY, NX, NZ, 2), ("y", "x", "z", "core"))
    rows, cols = ("y", "x"), ("z", "core")
    return jax.shard_map(
        per_device,
        mesh=fine,
        in_specs=(P(rows, None, cols), P(rows, cols, None, None), P(), P(), P()),
        out_specs=P(rows, None, cols),
        check_vma=False,
    )
```

```python
import functools

import jax
import jax.numpy as jnp
from jax import lax
from jax.experimental import pallas as pl
from jax.experimental.pallas import tpu as pltpu
from jax.sharding import Mesh, PartitionSpec as P

F32 = jnp.float32
BF16 = jnp.bfloat16
I32 = jnp.int32

C = 36
D = 36
PD = 32
NY = NX = 4
NR = NY * NX
NZ = 8
SLAB = 3
NV = 576
PAIRS = 512
NO = 60
CP = 40
K = D * CP
KP = 1536
FITS = ((5, 1), (5, 2), (6, 2), (9, 3))

SMEM = pl.BlockSpec(memory_space=pltpu.SMEM)
VMEM = pl.BlockSpec(memory_space=pltpu.VMEM)
HBM = pl.BlockSpec(memory_space=pltpu.HBM)


def in_hbm(x):
    return pltpu.with_memory_space_constraint(x, pltpu.HBM)


def labels_kernel(occ_ref, virt_ref, pairs_ref, row_ref, sym_ref, slot_ref, which_ref):
    pairs = pairs_ref[...]
    found = jnp.zeros_like(pairs)
    for o in range(NO):
        found = jnp.where(pairs == o, occ_ref[o], found)
    sym_ref[...] = jnp.bitwise_xor(found[0:1], found[1:2])

    labels = jnp.concatenate([row_ref[...], row_ref[:, 0:64]], axis=1)
    lane = lax.broadcasted_iota(I32, labels.shape, 1)
    at = lax.rem(lane, D)
    place = jnp.zeros_like(labels)
    for k in range(1, D):
        same = pltpu.roll(labels, k, 1) == labels
        place = place + (same & (at >= k)).astype(I32)
    top = jnp.max(jnp.where(lane < NV, place, 0))
    deep = jnp.maximum(slab_slot(virt_ref, jnp.int32(1)), slab_slot(virt_ref, jnp.int32(2)))
    which = jnp.int32(len(FITS) - 1)
    for i, (tiles, slots) in reversed(list(enumerate(FITS[:-1]))):
        which = jnp.where((top < 4 * tiles) & (deep < slots), i, which)
    which_ref[0] = which
    slot_ref[...] = jnp.where(which < len(FITS) - 1, place, at)[:, 0:NV]


def slab_slot(virt_ref, a):
    first = (a > 0) & (virt_ref[0] == virt_ref[a])
    second = (a > 1) & (virt_ref[1] == virt_ref[a])
    return first.astype(I32) + second.astype(I32)


def label_all(occ_irrep, virt_irrep, pairs, virt_row):
    return pl.pallas_call(
        labels_kernel,
        out_shape=[
            jax.ShapeDtypeStruct((1, PAIRS), I32),
            jax.ShapeDtypeStruct((1, NV), I32),
            jax.ShapeDtypeStruct((1,), I32),
        ],
        in_specs=[SMEM, SMEM, VMEM, VMEM],
        out_specs=[VMEM, VMEM, SMEM],
        name="label_all",
    )(occ_irrep, virt_irrep, pairs, virt_row)


def own_column(at_ref, sym_ref):
    pair = at_ref[0] * PD + lax.broadcasted_iota(I32, (PD, PAIRS), 0)
    mine = lax.broadcasted_iota(I32, (PD, PAIRS), 1) == pair
    return jnp.sum(jnp.where(mine, sym_ref[...], 0), axis=1, keepdims=True)


def pack_kernel(tiles, at_ref, virt_ref, slot_ref, x_hbm, cl_ref, sym_ref, o_hbm, x_buf, f_buf, t_buf, o_buf, in_sems, out_sems):
    def fetch(q):
        return pltpu.make_async_copy(x_hbm.at[pl.ds(4 * q, 4)], x_buf.at[pl.ds(4 * q, 4)], in_sems.at[q])

    for q in range(D // 4):
        fetch(q).start()
    f_buf[...] = jnp.zeros_like(f_buf)
    sym = own_column(at_ref, sym_ref)
    first = at_ref[1] * D

    @pl.loop(0, D // 4)
    def _(q):
        fetch(q).wait()
        for i in range(4):
            d = 4 * q + i
            keep = jnp.bitwise_xor(cl_ref[...], virt_ref[first + d]) == sym
            at = slot_ref[0, first + d]
            f_buf[at] = f_buf[at] + jnp.where(keep, x_buf[d], 0.0)

    for q in range(tiles):
        t_buf[q % 2] = f_buf[4 * q:4 * q + 4].reshape(4 * PD, NV).T
        for r in range(NR):
            o_buf[r, q * C:(q + 1) * C, :] = t_buf[q % 2, r * C:(r + 1) * C, :]
    out = []
    for r in range(NR):
        copy = pltpu.make_async_copy(o_buf.at[r], o_hbm.at[r], out_sems.at[r])
        copy.start()
        out.append(copy)
    for copy in out:
        copy.wait()


def pack_amplitudes(tiles, at, virt, slots, amps, cl, sym):
    block = (NR, tiles * C, 128)
    return pl.pallas_call(
        functools.partial(pack_kernel, tiles),
        out_shape=pltpu.HBM(block, F32),
        in_specs=[SMEM, SMEM, SMEM, HBM, VMEM, VMEM],
        out_specs=HBM,
        scratch_shapes=[
            pltpu.VMEM((D, PD, NV), F32),
            pltpu.VMEM((4 * tiles, PD, NV), F32),
            pltpu.VMEM((2, NV, 128), F32),
            pltpu.VMEM(block, F32),
            pltpu.SemaphoreType.DMA((D // 4,)),
            pltpu.SemaphoreType.DMA((NR,)),
        ],
        compiler_params=pltpu.CompilerParams(vmem_limit_bytes=20 << 20),
        name="pack_amplitudes",
    )(at, virt, slots, in_hbm(amps), cl, sym)


STEP = 6


def integrals_kernel(v_hbm, hi_hbm, lo_hbm, v_buf, h_buf, l_buf, in_sems, out_sems):
    def fetch(d, a):
        return pltpu.make_async_copy(v_hbm.at[:, a, d], v_buf.at[d, a], in_sems.at[d, a])

    @pl.loop(0, D)
    def _(d):
        for a in range(SLAB):
            fetch(d, a).start()

    zero = jnp.zeros((CP - C, NV), F32)
    for a in range(SLAB):
        h_buf[a, K:, :] = jnp.zeros((KP - K, NV), BF16)
        l_buf[a, K:, :] = jnp.zeros((KP - K, NV), BF16)
    out = []
    for i in range(D // STEP):
        @pl.loop(i * STEP // 2, (i + 1) * STEP // 2)
        def _(pair):
            d = 2 * pair
            at = pl.multiple_of(pair * 2 * CP, 16)
            for a in range(SLAB):
                fetch(d, a).wait()
                fetch(d + 1, a).wait()
                x = jnp.concatenate([v_buf[d, a], zero, v_buf[d + 1, a], zero], axis=0)
                h = x.astype(BF16)
                h_buf[a, pl.ds(at, 2 * CP), :] = h
                l_buf[a, pl.ds(at, 2 * CP), :] = (x - h.astype(F32)).astype(BF16)

        rows = pl.ds(i * STEP * CP, STEP * CP if (i + 1) * STEP < D else KP - i * STEP * CP)
        for n, (buf, hbm) in enumerate(((h_buf, hi_hbm), (l_buf, lo_hbm))):
            copy = pltpu.make_async_copy(buf.at[:, rows], hbm.at[:, rows], out_sems.at[n, i])
            copy.start()
            out.append(copy)
    for copy in out:
        copy.wait()


def split_integrals(v_t):
    block = (SLAB, KP, NV)
    return pl.pallas_call(
        integrals_kernel,
        out_shape=[pltpu.HBM(block, BF16)] * 2,
        in_specs=[HBM],
        out_specs=[HBM] * 2,
        scratch_shapes=[
            pltpu.VMEM((D, SLAB, C, NV), F32),
            pltpu.VMEM(block, BF16),
            pltpu.VMEM(block, BF16),
            pltpu.SemaphoreType.DMA((D, SLAB)),
            pltpu.SemaphoreType.DMA((2, D // STEP)),
        ],
        compiler_params=pltpu.CompilerParams(vmem_limit_bytes=28 << 20),
        cost_estimate=pl.CostEstimate(flops=20_000_000, bytes_accessed=36_000_000, transcendentals=0),
        name="split_integrals",
    )(in_hbm(v_t))


def regroup(blocks):
    lane = lax.broadcasted_iota(I32, blocks[0].shape, 1) // 32
    out = []
    for i in range(4):
        total = None
        for s in range(4):
            piece = blocks[s] if s == i else pltpu.roll(blocks[s], (32 * (s - i)) % 128, 1)
            total = piece if total is None else jnp.where(lane == s, piece, total)
        out.append(total)
    return out


def tn_dot(x, y):
    return lax.dot_general(x, y, (((0,), (0,)), ((), ())), preferred_element_type=F32)


def products_kernel(slots, at_ref, virt_ref, slot_ref, r_ref, sym_ref, cl_ref, bl_ref, vh_hbm, vl_hbm,
                    own_ref, away_ref, f_buf, h_buf, l_buf, t_buf, vh_ref, vl_ref, sems):
    def fetch(a, n):
        hbm, buf = ((vh_hbm, vh_ref), (vl_hbm, vl_ref))[n]
        return pltpu.make_async_copy(hbm.at[a], buf.at[a], sems.at[a, n])

    for a in range(SLAB):
        for n in range(2):
            fetch(a, n).start()
    first = at_ref[1] * D
    h_buf[K:, :] = jnp.zeros((KP - K, PAIRS), BF16)
    l_buf[K:, :] = jnp.zeros((KP - K, PAIRS), BF16)
    zero = jnp.zeros((CP - C, 128), F32)
    tiles = r_ref.shape[1] // C

    @pl.loop(0, NY)
    def _(y):
        for q in range(tiles):
            blocks = [jnp.concatenate([r_ref[4 * y + s, q * C:(q + 1) * C, :], zero], axis=0) for s in range(4)]
            for i, x in enumerate(regroup(blocks)):
                f_buf[y, 4 * q + i] = x

    @pl.loop(0, D // 2)
    def _(pair):
        d = 2 * pair
        at = pl.multiple_of(pair * 2 * CP, 16)
        for y in range(NY):
            cut = slice(y * 128, (y + 1) * 128)
            labels = jnp.bitwise_xor(cl_ref[...], sym_ref[:, cut])
            parts = [jnp.where(labels == virt_ref[first + e], f_buf[y, slot_ref[0, first + e]], 0.0) for e in (d, d + 1)]
            x = jnp.concatenate(parts, axis=0)
            h = x.astype(BF16)
            h_buf[pl.ds(at, 2 * CP), cut] = h
            l_buf[pl.ds(at, 2 * CP), cut] = (x - h.astype(F32)).astype(BF16)

    if slots < SLAB:
        t_buf[...] = jnp.zeros_like(t_buf)

    @pl.loop(0, SLAB)
    def _(a):
        fetch(a, 0).wait()
        fetch(a, 1).wait()
        out = tn_dot(vh_ref[a], h_buf[...])
        out += tn_dot(vh_ref[a], l_buf[...])
        out += tn_dot(vl_ref[a], h_buf[...])
        if slots < SLAB:
            at = slab_slot(virt_ref, a)
            for y in range(NY):
                cut = slice(y * 128, (y + 1) * 128)
                keep = jnp.bitwise_xor(bl_ref[...], virt_ref[a]) == sym_ref[:, cut]
                t_buf[at, :, cut] = t_buf[at, :, cut] + jnp.where(keep, out[:, cut], 0.0)
        else:
            t_buf[a] = out

    for flag in range(2):
        @pl.when(at_ref[2] == flag)
        def _():
            for j in range(2 * NZ):
                o_ref = own_ref if j % 2 == flag else away_ref
                for t in range(slots):
                    o_ref[j // 2, t * 36:(t + 1) * 36, :] = t_buf[t, j * 36:(j + 1) * 36, :]


def products(slots, at, virt, dslots, recv, sym, cl, bl, vh, vl):
    block = jax.ShapeDtypeStruct((NZ, slots * 36, PAIRS), F32)
    folded = recv.shape[1] // C * 4
    return pl.pallas_call(
        functools.partial(products_kernel, slots),
        out_shape=[block, block],
        in_specs=[SMEM] * 3 + [VMEM] * 4 + [HBM] * 2,
        out_specs=[VMEM] * 2,
        scratch_shapes=[
            pltpu.VMEM((NY, folded, CP, 128), F32),
            pltpu.VMEM((KP, PAIRS), BF16),
            pltpu.VMEM((KP, PAIRS), BF16),
            pltpu.VMEM((slots, NV, PAIRS), F32),
            pltpu.VMEM((SLAB, KP, NV), BF16),
            pltpu.VMEM((SLAB, KP, NV), BF16),
            pltpu.SemaphoreType.DMA((SLAB, 2)),
        ],
        compiler_params=pltpu.CompilerParams(vmem_limit_bytes=34 << 20),
        cost_estimate=pl.CostEstimate(flops=2 * 3 * NV * SLAB * KP * PAIRS, bytes_accessed=10_000_000, transcendentals=0),
        name="products",
    )(at, virt, dslots, recv, sym, cl, bl, in_hbm(vh), in_hbm(vl))


def pair_kernel(slots, own_ref, other_ref, o_hbm, o_buf, sems):
    jb = slots * 36

    def put(r):
        return pltpu.make_async_copy(o_buf.at[r], o_hbm.at[r], sems.at[r])

    for y in range(NY):
        cut = slice(y * 128, (y + 1) * 128)
        for h in range(2):
            blocks = [own_ref[2 * rb + h, 0:jb, cut] + other_ref[2 * rb + h, 0:jb, cut] for rb in range(4)]
            for x, block in enumerate(regroup(blocks)):
                o_buf[4 * y + x, h * jb:(h + 1) * jb, :] = block
        for x in range(NX):
            put(4 * y + x).start()
    for r in range(NR):
        put(r).wait()


def sum_pair(slots, own, other):
    block = (NR, 2 * slots * 36, 128)
    return pl.pallas_call(
        functools.partial(pair_kernel, slots),
        out_shape=pltpu.HBM(block, F32),
        in_specs=[VMEM] * 2,
        out_specs=HBM,
        scratch_shapes=[pltpu.VMEM(block, F32), pltpu.SemaphoreType.DMA((NR,))],
        compiler_params=pltpu.CompilerParams(vmem_limit_bytes=8 << 20),
        name="sum_pair",
    )(own, other)


def row_kernel(slots, x_ref, o_ref):
    jb = slots * 36
    total = x_ref[0]
    for s in range(1, NR):
        total = total + x_ref[s]
    zero = jnp.zeros((128 - jb, 128), F32)
    for h in range(2):
        turned = jnp.concatenate([total[h * jb:(h + 1) * jb, :], zero], axis=0).T
        for rb in range(4):
            o_ref[2 * rb + h] = turned[rb * 32:(rb + 1) * 32, :]


def sum_row(slots, x):
    return pl.pallas_call(
        functools.partial(row_kernel, slots),
        out_shape=jax.ShapeDtypeStruct((NZ, PD, 128), F32),
        in_specs=[VMEM],
        out_specs=VMEM,
        compiler_params=pltpu.CompilerParams(vmem_limit_bytes=8 << 20),
        name="sum_row",
    )(x)


def last_kernel(slots, at_ref, virt_ref, x_ref, sym_ref, lab_ref, o_ref):
    total = x_ref[0]
    for s in range(1, NZ):
        total = total + x_ref[s]
    sym = own_column(at_ref, sym_ref)
    for a in range(SLAB):
        at = slab_slot(virt_ref, jnp.int32(a)) if slots < SLAB else a
        x = total[:, 0:36]
        for t in range(1, slots):
            x = jnp.where(at == t, total[:, t * 36:(t + 1) * 36], x)
        keep = jnp.bitwise_xor(lab_ref[...], virt_ref[a]) == sym
        o_ref[a] = jnp.where(keep, x, 0.0)


def sum_last(slots, at, virt, x, sym, lab):
    return pl.pallas_call(
        functools.partial(last_kernel, slots),
        out_shape=jax.ShapeDtypeStruct((SLAB, PD, 36), F32),
        in_specs=[SMEM] * 2 + [VMEM] * 3,
        out_specs=VMEM,
        compiler_params=pltpu.CompilerParams(vmem_limit_bytes=8 << 20),
        name="sum_last",
    )(at, virt, x, sym, lab)


def ladder(tiles, slots, amps_t, v_t, virt, virt_row, sym, dslots, at):
    labels_c = lax.dynamic_slice_in_dim(virt, at[0] * C, C)
    lab = lax.dynamic_slice_in_dim(virt, at[1] * D, D).reshape(1, D)
    cl = jnp.broadcast_to(jnp.pad(labels_c, (0, CP - C))[:, None], (CP, 128))
    bl = jnp.broadcast_to(virt[:, None], (NV, 128))

    sent = pack_amplitudes(tiles, at, virt, dslots, amps_t, virt_row, sym)
    recv = lax.all_to_all(sent, ("y", "x"), 0, 0, tiled=True)
    vh, vl = split_integrals(v_t)
    own, away = products(slots, at, virt, dslots, recv, sym, cl, bl, vh, vl)
    other = lax.ppermute(away, "core", [(0, 1), (1, 0)])
    by_row = lax.all_to_all(sum_pair(slots, own, other), ("y", "x"), 0, 0, tiled=True)
    by_z = lax.all_to_all(sum_row(slots, by_row), "z", 0, 0, tiled=True)
    return sum_last(slots, at, virt, by_z, sym, lab)


def per_device(amplitudes, integrals, virt_irrep, occ_irrep, pair_index):
    row_at = lax.axis_index("y") * NX + lax.axis_index("x")
    core_at = lax.axis_index("core")
    at = jnp.stack([row_at, lax.axis_index("z") * 2 + core_at, core_at]).astype(I32)
    amps_t = jnp.transpose(amplitudes, (2, 0, 1))
    v_t = jnp.transpose(integrals, (0, 2, 1, 3))
    virt_row = virt_irrep.reshape(1, NV)
    sym, dslots, which = label_all(occ_irrep, virt_irrep, pair_index.T, virt_row)
    programs = [functools.partial(ladder, tiles, slots) for tiles, slots in FITS]
    out = lax.switch(which[0], programs, amps_t, v_t, virt_irrep, virt_row, sym, dslots, at)
    return jnp.transpose(out, (1, 0, 2))


def solution(mesh):
    fine = Mesh(mesh.devices.reshape(NY, NX, NZ, 2), ("y", "x", "z", "core"))
    rows, cols = ("y", "x"), ("z", "core")
    return jax.shard_map(
        per_device,
        mesh=fine,
        in_specs=(P(rows, None, cols), P(rows, cols, None, None), P(), P(), P()),
        out_specs=P(rows, None, cols),
        check_vma=False,
    )
```
